256 devices in a mesh: mid: 16 (over y, z_lo, core), leaf: 16 (over x, z_hi).
Axes of the slice: x: 4, y: 4, z: 8 (z_hi: 4, z_lo: 2; z = z_hi * 2 + z_lo), core: 2. Of those that a mesh axis runs over, the one named last changes fastest.
Arguments:
- queries: bfloat16 [65536, 4096], P(('mid', 'leaf')), may hold values from -128 to 128
- out_grad: bfloat16 [65536, 4096], P(('mid', 'leaf')), may hold values from -6 to 6
- leaf_keys: bfloat16 [65536, 1024], P(('mid', 'leaf')), may hold values from -6 to 6
- leaf_values: bfloat16 [65536, 1024], P(('mid', 'leaf')), may hold values from -6 to 6
- mid_keys: bfloat16 [4096, 1024], P(('mid', 'leaf')), may hold values from -6 to 6
- mid_values: bfloat16 [4096, 1024], P(('mid', 'leaf')), may hold values from -6 to 6
- root_keys: bfloat16 [512, 1024], P(('mid', 'leaf')), may hold values from -4 to 4
- root_values: bfloat16 [512, 1024], P(('mid', 'leaf')), may hold values from -6 to 6
- mid_len: int32 [16], P('mid'), may hold values from 1 to 256, 3072 in all
- leaf_len: int32 [256], P(('mid', 'leaf')), may hold values from 1 to 256, 40960 in all
Outputs:
- query_grad: bfloat16 [65536, 4096], P(('mid', 'leaf'))
- leaf_key_grad: bfloat16 [65536, 1024], P(('mid', 'leaf'))
- leaf_value_grad: bfloat16 [65536, 1024], P(('mid', 'leaf'))
- mid_key_grad: float32 [4096, 1024], P(('mid', 'leaf'))
- mid_value_grad: float32 [4096, 1024], P(('mid', 'leaf'))
- root_key_grad: float32 [512, 1024], P(('mid', 'leaf'))
- root_value_grad: float32 [512, 1024], P(('mid', 'leaf'))
The draws below stay inside these ranges and needn't reach their ends.
Inputs may be any that keep to these rules, and one draw needn't show every extreme that they name: `mid_len`: at least one mid branch has all 256 tokens live. `leaf_len`: at least one leaf has all 256 tokens live.
All inputs are finite; a program needn't handle non-finite values. No bound on the sum of `mid_len` or of `leaf_len` on one device may be relied on, other than what follows from the above.
Results may differ from the reference program's by a relative error of at most 0.013.
Values may be sent and summed in bfloat16 or wider, within the bound.
A program may use at most 128 MiB of HBM per device.

```python
import math
import jax
import jax.numpy as jnp
import numpy as np
from jax import lax

QH = 32
KVH = 8
HD = 128
LEAF = 256
BRANCHES = 16
BRANCH_LEAVES = 16
LEAVES = 256
MID = 256
ROOT = 512


def shared_root(key):
    return jnp.clip(jax.random.normal(jax.random.fold_in(key, 101), (ROOT, KVH * HD), jnp.float32), -4.0, 4.0)


def draw_root_keys(key, part):
    base_keys = shared_root(key)
    return base_keys.astype(jnp.bfloat16)


def draw_queries(key, part):
    key = jax.random.fold_in(key, 7)
    total_rows = LEAVES * LEAF
    drawn = jnp.clip(jax.random.normal(jax.random.fold_in(key, 1), (total_rows, QH * HD), jnp.float32), -4.0, 4.0)
    return drawn.astype(jnp.bfloat16)


def levels(stream_key, extent, split, smallest, largest):
    factor_of, own = 1.0, jax.random.fold_in(stream_key, 6)
    for axis_at, shards_of in split:
        steps = jnp.exp(jax.random.uniform(jax.random.fold_in(own, axis_at), (shards_of,), jnp.float32, smallest / len(split), largest / len(split)))
        factor_of = factor_of * jnp.repeat(steps, extent[axis_at] // shards_of).reshape([-1 if axis == axis_at else 1 for axis in range(len(extent))])
    return factor_of


def profile(amount, total, reach, skew):
    portions = [(1 << 20) // math.isqrt(grade ** skew) + 1 for grade in range(2, amount + 1)]
    surplus, holding = total - reach - (amount - 1), [1] * (amount - 1)
    while surplus > 0:
        candidates = [i for i in range(amount - 1) if holding[i] < reach]
        pool, remaining = sum([portions[i] for i in candidates]), surplus
        for i in candidates:
            addition = min(reach - holding[i], max(1, remaining * portions[i] // pool), surplus)
            holding[i] = holding[i] + addition
            surplus = surplus - addition
    return np.array([reach] + holding)


def ragged_sizes(own_key, number_of, total, reach, lean):
    if number_of == 2:
        one = jax.random.randint(own_key, (), max(1, total - reach), min(reach, total - 1) + 1)
        return jnp.stack([one, total - one])
    tallies = jnp.asarray(profile(number_of, total, reach, lean), jnp.int32)
    twos = (number_of - 1) // 2
    source_of, taker = tallies[1:1 + 2 * twos:2], tallies[2:2 + 2 * twos:2]
    room = jnp.minimum(source_of - 1, reach - taker)
    shifted = jax.random.randint(jax.random.fold_in(own_key, 1), (twos,), 0, 1 << 20) % (room + 1)
    tallies = tallies.at[1:1 + 2 * twos:2].set(source_of - shifted).at[2:2 + 2 * twos:2].set(taker + shifted)
    return tallies[jax.random.permutation(jax.random.fold_in(own_key, 2), number_of)]


def normal_values(stream_key, shape, deviation, most, cuts=(), kind=jnp.bfloat16):
    gain = levels(stream_key, shape, cuts, -0.22, 0.18) if cuts else 1.0
    values = jax.random.normal(stream_key, shape, jnp.float32) * deviation * gain
    return jnp.minimum(jnp.maximum(values, -most), most).astype(kind)


def setup_inputs(seed: int = 0) -> dict:
    arg_keys = jax.random.split(jax.random.key(seed), 11)
    queries = draw_queries(jax.random.fold_in(arg_keys[10], 71), 0)
    out_grad = normal_values(arg_keys[1], (LEAVES * LEAF, QH * HD), 1.0, 6.0, ((0, 256),))
    leaf_keys = normal_values(arg_keys[2], (LEAVES * LEAF, KVH * HD), 1.0, 6.0, ((0, 256),))
    leaf_values = normal_values(arg_keys[3], (LEAVES * LEAF, KVH * HD), 1.0, 6.0, ((0, 256),))
    mid_keys = normal_values(arg_keys[4], (BRANCHES * MID, KVH * HD), 1.0, 6.0, ((0, 256),))
    mid_values = normal_values(arg_keys[5], (BRANCHES * MID, KVH * HD), 1.0, 6.0, ((0, 256),))
    root_keys = draw_root_keys(jax.random.fold_in(arg_keys[10], 71), 0)
    root_values = normal_values(arg_keys[7], (ROOT, KVH * HD), 1.0, 6.0, ((0, 256),))
    mid_len = ragged_sizes(arg_keys[8], BRANCHES, BRANCHES * MID * 3 // 4, MID, 1).astype(jnp.int32)
    leaf_len = ragged_sizes(arg_keys[9], LEAVES, LEAVES * LEAF * 5 // 8, LEAF, 1).astype(jnp.int32)
    return {"queries": queries, "out_grad": out_grad, "leaf_keys": leaf_keys, "leaf_values": leaf_values, "mid_keys": mid_keys, "mid_values": mid_values, "root_keys": root_keys, "root_values": root_values, "mid_len": mid_len, "leaf_len": leaf_len}


def leaf_backward(queries, out_grad, all_keys, all_values, root_rows, mid_rows, mid_live, leaf_live):
    leaf_rows = queries.shape[0]
    key_rows = all_keys.shape[0]
    heads_per = QH // KVH
    span_cols = heads_per * HD
    column = jnp.arange(key_rows, dtype=jnp.int32)[None, :]
    row_ids = jnp.arange(leaf_rows, dtype=jnp.int32)[:, None]
    offset = root_rows + mid_rows
    leaf_pos = column - offset
    in_root = column < root_rows
    in_mid = (column >= root_rows) & (column < offset) & (column - root_rows < mid_live)
    in_leaf = (leaf_pos >= 0) & (leaf_pos <= row_ids) & (leaf_pos < leaf_live)
    allowed = in_root | in_mid | in_leaf
    live_rows = (jnp.arange(leaf_rows, dtype=jnp.int32) < leaf_live).astype(jnp.float32)[None, :, None]
    factor = HD ** -0.5
    query_wide = queries.astype(jnp.float32)
    grad_wide = out_grad.astype(jnp.float32)
    keys_wide = all_keys.astype(jnp.float32)
    values_wide = all_values.astype(jnp.float32)

    def one_head(head_index, buffers):
        query_acc, key_acc, value_acc = buffers
        query_part = lax.dynamic_slice_in_dim(query_wide, head_index * span_cols, span_cols, 1).reshape(leaf_rows, heads_per, HD)
        grad_part = lax.dynamic_slice_in_dim(grad_wide, head_index * span_cols, span_cols, 1).reshape(leaf_rows, heads_per, HD)
        key_part = lax.dynamic_slice_in_dim(keys_wide, head_index * HD, HD, 1)
        value_part = lax.dynamic_slice_in_dim(values_wide, head_index * HD, HD, 1)
        scores = factor * jnp.einsum("igd,jd->gij", query_part, key_part)
        scores = jnp.where(allowed[None], scores, -1e30)
        row_max = jnp.max(scores, axis=-1, keepdims=True)
        weights = jnp.exp(scores - row_max)
        probs = weights / jnp.sum(weights, axis=-1, keepdims=True) * live_rows
        probs_low = lax.optimization_barrier(probs.astype(jnp.bfloat16)).astype(jnp.float32)
        value_term = jnp.einsum("gij,igd->jd", probs_low, grad_part)
        dprobs = jnp.einsum("igd,jd->gij", grad_part, value_part)
        row_dots = jnp.sum(probs * dprobs, axis=-1, keepdims=True)
        dscores = lax.optimization_barrier((probs * (dprobs - row_dots)).astype(jnp.bfloat16)).astype(jnp.float32)
        query_term = factor * jnp.einsum("gij,jd->igd", dscores, key_part)
        key_term = factor * jnp.einsum("gij,igd->jd", dscores, query_part)
        query_acc = lax.dynamic_update_slice_in_dim(query_acc, query_term.reshape(leaf_rows, span_cols).astype(jnp.bfloat16), head_index * span_cols, 1)
        key_acc = lax.dynamic_update_slice_in_dim(key_acc, key_term, head_index * HD, 1)
        value_acc = lax.dynamic_update_slice_in_dim(value_acc, value_term, head_index * HD, 1)
        return query_acc, key_acc, value_acc

    start = (jnp.zeros((leaf_rows, QH * HD), jnp.bfloat16), jnp.zeros((key_rows, KVH * HD), jnp.float32), jnp.zeros((key_rows, KVH * HD), jnp.float32))
    return lax.fori_loop(0, KVH, one_head, start)


def reference(queries, out_grad, leaf_keys, leaf_values, mid_keys, mid_values, root_keys, root_values, mid_len, leaf_len):
    kv_cols = KVH * HD
    query_cols = QH * HD
    by_leaf = (queries.reshape(BRANCHES, BRANCH_LEAVES, LEAF, query_cols), out_grad.reshape(BRANCHES, BRANCH_LEAVES, LEAF, query_cols), leaf_keys.reshape(BRANCHES, BRANCH_LEAVES, LEAF, kv_cols), leaf_values.reshape(BRANCHES, BRANCH_LEAVES, LEAF, kv_cols), leaf_len.reshape(BRANCHES, BRANCH_LEAVES))
    by_branch = (mid_keys.reshape(BRANCHES, MID, kv_cols), mid_values.reshape(BRANCHES, MID, kv_cols), mid_len)

    def branch_step(root_totals, items):
        leaf_items = items[:5]
        branch_keys, branch_values, branch_live = items[5], items[6], items[7]

        def leaf_step(totals, piece):
            query_part, grad_part, own_keys, own_values, own_live = piece
            all_keys = jnp.concatenate([root_keys, branch_keys, own_keys], 0)
            all_values = jnp.concatenate([root_values, branch_values, own_values], 0)
            query_out, key_terms, value_terms = leaf_backward(query_part, grad_part, all_keys, all_values, ROOT, MID, branch_live, own_live)
            totals = (totals[0] + key_terms[ROOT:ROOT + MID], totals[1] + value_terms[ROOT:ROOT + MID], totals[2] + key_terms[:ROOT], totals[3] + value_terms[:ROOT])
            return totals, (query_out, key_terms[ROOT + MID:].astype(jnp.bfloat16), value_terms[ROOT + MID:].astype(jnp.bfloat16))

        start = (jnp.zeros((MID, kv_cols), jnp.float32), jnp.zeros((MID, kv_cols), jnp.float32), jnp.zeros((ROOT, kv_cols), jnp.float32), jnp.zeros((ROOT, kv_cols), jnp.float32))
        totals, leaf_outs = lax.scan(leaf_step, start, leaf_items)
        root_totals = (root_totals[0] + totals[2], root_totals[1] + totals[3])
        return root_totals, (leaf_outs[0], leaf_outs[1], leaf_outs[2], totals[0], totals[1])

    start_root = (jnp.zeros((ROOT, kv_cols), jnp.float32), jnp.zeros((ROOT, kv_cols), jnp.float32))
    root_totals, stacked = lax.scan(branch_step, start_root, by_leaf + by_branch)
    query_grad = stacked[0].reshape(LEAVES * LEAF, query_cols)
    leaf_key_grad = stacked[1].reshape(LEAVES * LEAF, kv_cols)
    leaf_value_grad = stacked[2].reshape(LEAVES * LEAF, kv_cols)
    mid_key_grad = stacked[3].reshape(BRANCHES * MID, kv_cols)
    mid_value_grad = stacked[4].reshape(BRANCHES * MID, kv_cols)
    return (query_grad, leaf_key_grad, leaf_value_grad, mid_key_grad, mid_value_grad, root_totals[0], root_totals[1])
```

```python
import functools

import jax
import jax.numpy as jnp
from jax import lax
from jax.experimental import pallas as pl
from jax.experimental.pallas import tpu as pltpu
from jax.sharding import PartitionSpec as P

QH = 32
KVH = 8
HD = 128
GROUP = QH // KVH
LEAF = 256
MID = 256
ROOT = 512
KEYS = ROOT + MID + LEAF
HALF = ROOT // 2
OWN = ROOT + MID
CHUNK = 64
AHEAD = 2
FACTOR = HD ** (-0.5)
LOG2E = 1.4426950408889634
MESH = pl.DeviceIdType.MESH
BF = jnp.bfloat16
F32 = jnp.float32


def nt(a, b):
    return lax.dot_general(a, b, (((1,), (1,)), ((), ())), preferred_element_type=F32)


def tn(a, b):
    return lax.dot_general(a, b, (((0,), (0,)), ((), ())), preferred_element_type=F32)


def kernel(
    mid_len, leaf_len, rk, rv, mk, mv, q_hbm, g_hbm, lk_hbm, lv_hbm,
    dq_hbm, dlk_hbm, dlv_hbm, dmk, dmv, drk, drv,
    kv, qb, gb, dqb, dlk, dlv, bias_mid, bias_own, live, s_scr, dp_scr, p_scr, ds_scr,
    shard, gd, gf, rsend, recv_a, bsend, recv_b, msend, recv_x, zsend, recv_z, df, dsend, recv_d,
    load_q, load_g, load_kv, store_sem,
    gd_send, gd_recv, gb_send, gb_recv, ga_send, ga_recv, gz_send, gz_recv, gx_send, gx_recv,
    ra_send, ra_recv, rb_send, rb_recv, rd_send, rd_recv, rx_send, rx_recv, rz_send, rz_recv,
):
    m = lax.axis_index("mid")
    l = lax.axis_index("leaf")
    core = lax.rem(m, 2)
    b = m // 2
    x = l // 4
    z = lax.rem(l, 4)

    def at(mm, ll):
        return {"mid": mm, "leaf": ll}

    sibling = at(m + 1 - 2 * core, l)

    def leaf_peer(d):
        return lax.rem(l + d, 16)

    def b_peer(d):
        return lax.rem(b + d, 8)

    def x_peer(d):
        return lax.rem(x + d, 4)

    def z_peer(d):
        return lax.rem(z + d, 4)

    def send(src, dst, ssem, rsem, device):
        pltpu.make_async_remote_copy(
            src_ref=src, dst_ref=dst, send_sem=ssem, recv_sem=rsem,
            device_id=device, device_id_type=MESH,
        ).start()

    def wait(ref, sem):
        pltpu.make_async_copy(ref, ref, sem).wait()

    def cols(h, width):
        return pl.ds(pl.multiple_of(h * width, width), width)

    for h in range(KVH):
        pltpu.make_async_copy(lk_hbm.at[:, cols(h, HD)], kv.at[h, 0, pl.ds(OWN, LEAF), :], load_kv.at[h]).start()
        pltpu.make_async_copy(lv_hbm.at[:, cols(h, HD)], kv.at[h, 1, pl.ds(OWN, LEAF), :], load_kv.at[h]).start()
        w = GROUP * HD
        pltpu.make_async_copy(q_hbm.at[:, cols(h, w)], qb.at[:, cols(h, w)], load_q.at[h]).start()
        pltpu.make_async_copy(g_hbm.at[:, cols(h, w)], gb.at[:, cols(h, w)], load_g.at[h]).start()

    barrier = pltpu.get_barrier_semaphore()
    for d in range(1, 16):
        pl.semaphore_signal(barrier, inc=1, device_id=at(m, leaf_peer(d)), device_id_type=MESH)
    for d in range(1, 8):
        pl.semaphore_signal(barrier, inc=1, device_id=at(b_peer(d) * 2 + core, l), device_id_type=MESH)
    pl.semaphore_signal(barrier, inc=1, device_id=sibling, device_id_type=MESH)

    for kind, ref in ((0, rk), (1, rv)):
        val = ref[...].astype(F32)
        for r in range(2):
            for h in range(KVH):
                gf[kind, pl.ds(r * KVH + h, 1), :] = val[r : r + 1, h * HD : (h + 1) * HD]
        shard[kind] = gf[kind, pl.ds(0, 16), :].astype(BF)
        gd[l, kind] = shard[kind]
    mid_rows = pl.ds(pl.multiple_of(ROOT + l * 16, 16), 16)
    for kind, ref in ((0, mk), (1, mv)):
        for h in range(KVH):
            kv[h, kind, mid_rows, :] = ref[:, h * HD : (h + 1) * HD]

    pl.semaphore_wait(barrier, 23)

    for d in range(1, 16):
        send(shard, gd.at[l], gd_send, gd_recv, at(m, leaf_peer(d)))
    for h in range(KVH):
        for d in range(1, 4):
            part = kv.at[h, :, mid_rows, :]
            send(part, part, gz_send, gz_recv.at[h], at(m, x * 4 + z_peer(d)))

    mlen = mid_len[0]
    llen = leaf_len[0]
    bias_mid[...] = jnp.where(lax.broadcasted_iota(jnp.int32, (8, MID), 1) < mlen, 0.0, -1e30)
    row = lax.broadcasted_iota(jnp.int32, (LEAF, LEAF), 0)
    col = lax.broadcasted_iota(jnp.int32, (LEAF, LEAF), 1)
    bias_own[...] = jnp.where((col <= row) & (col < llen), 0.0, -1e30)
    live[...] = jnp.where(lax.broadcasted_iota(jnp.int32, (LEAF, HD), 0) < llen, 1.0, 0.0)

    my_rows = pl.ds(pl.multiple_of(core * HALF + b * 32, 32), 32)
    my_half = pl.ds(pl.multiple_of(core * HALF, HALF), HALF)
    other_half = pl.ds(pl.multiple_of((1 - core) * HALF, HALF), HALF)
    x_rows = pl.ds(pl.multiple_of(ROOT + x * 64, 64), 64)

    wait(gd.at[pl.ds(0, 15)], gd_recv)
    for kind in range(2):
        gf[kind] = gd[:, kind].reshape(256, HD).astype(F32)
    for h in range(KVH):
        for kind in range(2):
            kv[h, kind, my_rows, :] = gf[kind, pl.ds(h, 32, stride=KVH), :].astype(BF)
        for d in range(1, 8):
            part = kv.at[h, :, my_rows, :]
            send(part, part, gb_send, gb_recv.at[h], at(b_peer(d) * 2 + core, l))

    def pass_on(h):
        wait(kv.at[h, :, pl.ds(0, 224), :], gb_recv.at[h])
        part = kv.at[h, :, my_half, :]
        send(part, part, ga_send, ga_recv.at[h], sibling)
        wait(kv.at[h, :, pl.ds(ROOT, 48), :], gz_recv.at[h])
        for d in range(1, 4):
            part = kv.at[h, :, x_rows, :]
            send(part, part, gx_send, gx_recv.at[h], at(m, x_peer(d) * 4 + z))

    for h in range(AHEAD):
        pass_on(h)

    def compute(h):
        keys = kv.at[h, 0]
        values = kv.at[h, 1]

        def head_cols(g):
            return pl.ds(pl.multiple_of(h * (GROUP * HD) + g * HD, HD), HD)

        def dots(g):
            s_scr[g] = nt(qb[:, head_cols(g)], keys[...])
            dp_scr[g] = nt(gb[:, head_cols(g)], values[...])

        def soft(g):
            for r0 in range(0, LEAF, CHUNK):
                rows = pl.ds(r0, CHUNK)
                out = pl.ds(g * LEAF + r0, CHUNK)
                s = s_scr[g, rows, :] * (FACTOR * LOG2E)
                s = jnp.concatenate(
                    [s[:, :ROOT], s[:, ROOT:OWN] + bias_mid[0:1, :], s[:, OWN:] + bias_own[rows, :]], 1
                )
                top = jnp.max(s, -1, keepdims=True)
                w = jnp.exp2(s - top)
                p = w * (live[rows, 0:1] / jnp.sum(w, -1, keepdims=True))
                p_scr[out, :] = p.astype(BF)
                dp = dp_scr[g, rows, :]
                dot = jnp.sum(p * dp, -1, keepdims=True)
                ds_scr[out, :] = (p * (dp - dot)).astype(BF)
            dq = jnp.dot(ds_scr[pl.ds(g * LEAF, LEAF), :], keys[...], preferred_element_type=F32)
            dqb[:, head_cols(g)] = (dq * FACTOR).astype(BF)

        dots(0)
        for g in range(GROUP):
            if g + 1 < GROUP:
                dots(g + 1)
            soft(g)
        w = GROUP * HD
        pltpu.make_async_copy(dqb.at[:, cols(h, w)], dq_hbm.at[:, cols(h, w)], store_sem.at[0]).start()
        qs = jnp.concatenate([qb[:, head_cols(g)] for g in range(GROUP)], 0)
        gs = jnp.concatenate([gb[:, head_cols(g)] for g in range(GROUP)], 0)
        dk = tn(qs, ds_scr[...]).T * FACTOR
        dv = tn(gs, p_scr[...]).T
        for kind, val, own in ((0, dk, dlk), (1, dv, dlv)):
            low = val.astype(BF)
            rsend[h, kind] = low[:ROOT]
            msend[h, kind] = low[ROOT:OWN]
            own[:, cols(h, HD)] = low[OWN:]

    def first_sends(h):
        send(rsend.at[h, :, other_half, :], recv_a.at[h], ra_send, ra_recv.at[h], sibling)
        for d in range(1, 4):
            xp = x_peer(d)
            src = msend.at[h, :, pl.ds(pl.multiple_of(xp * 64, 64), 64), :]
            send(src, recv_x.at[h, d - 1], rx_send, rx_recv.at[h], at(m, xp * 4 + z))

    def second_sends(h):
        wait(recv_a.at[h], ra_recv.at[h])
        bsend[h] = (rsend[h, :, my_half, :].astype(F32) + recv_a[h].astype(F32)).astype(BF)
        for d in range(1, 8):
            bp = b_peer(d)
            src = bsend.at[h, :, pl.ds(pl.multiple_of(bp * 32, 32), 32), :]
            send(src, recv_b.at[h, d - 1], rb_send, rb_recv.at[h], at(bp * 2 + core, l))
        wait(recv_x.at[h], rx_recv.at[h])
        own = msend[h, :, pl.ds(pl.multiple_of(x * 64, 64), 64), :].astype(F32)
        zsend[h] = (own + jnp.sum(recv_x[h].astype(F32), 0)).astype(BF)
        for d in range(1, 4):
            zp = z_peer(d)
            src = zsend.at[h, :, pl.ds(pl.multiple_of(zp * 16, 16), 16), :]
            send(src, recv_z.at[h, d - 1], rz_send, rz_recv.at[h], at(m, x * 4 + zp))

    def third_sums(h):
        wait(recv_b.at[h], rb_recv.at[h])
        own = bsend[h, :, pl.ds(pl.multiple_of(b * 32, 32), 32), :].astype(F32)
        total = own + jnp.sum(recv_b[h].astype(F32), 0)
        for kind in range(2):
            df[kind, pl.ds(h, 32, stride=KVH), :] = total[kind]
        wait(recv_z.at[h], rz_recv.at[h])
        own = zsend[h, :, pl.ds(pl.multiple_of(z * 16, 16), 16), :].astype(F32)
        total = own + jnp.sum(recv_z[h].astype(F32), 0)
        dmk[:, cols(h, HD)] = total[0]
        dmv[:, cols(h, HD)] = total[1]

    def step(h, carry):
        @pl.when(h + AHEAD < KVH)
        def _():
            pass_on(h + AHEAD)

        wait(qb.at[:, cols(h, GROUP * HD)], load_q.at[h])
        wait(gb.at[:, cols(h, GROUP * HD)], load_g.at[h])
        wait(kv.at[h, :, pl.ds(OWN, LEAF), :], load_kv.at[h])
        wait(kv.at[h, :, pl.ds(0, HALF), :], ga_recv.at[h])
        wait(kv.at[h, :, pl.ds(0, 192), :], gx_recv.at[h])
        compute(h)
        first_sends(h)

        @pl.when(h >= 1)
        def _():
            second_sends(h - 1)

        @pl.when(h >= 2)
        def _():
            third_sums(h - 2)

        return carry

    lax.fori_loop(0, KVH, step, 0)
    out_k = pltpu.make_async_copy(dlk, dlk_hbm, store_sem.at[1])
    out_v = pltpu.make_async_copy(dlv, dlv_hbm, store_sem.at[2])
    out_k.start()
    out_v.start()
    second_sends(KVH - 1)
    third_sums(KVH - 2)
    third_sums(KVH - 1)

    for kind in range(2):
        dsend[:, kind] = df[kind].astype(BF).reshape(16, 16, HD)
    for d in range(1, 16):
        lp = leaf_peer(d)
        send(dsend.at[lp], recv_d.at[d - 1], rd_send, rd_recv, at(m, lp))
    wait(recv_d, rd_recv)
    total = dsend[l].astype(F32) + jnp.sum(recv_d[...].astype(F32), 0)
    for kind, ref in ((0, drk), (1, drv)):
        for r in range(2):
            for h in range(KVH):
                ref[r : r + 1, h * HD : (h + 1) * HD] = total[kind, r * KVH + h : r * KVH + h + 1]

    wait(dqb, store_sem.at[0])
    out_k.wait()
    out_v.wait()
    wait(gd.at[pl.ds(0, 15)], gd_send)
    wait(kv.at[:, :, pl.ds(0, 224), :], gb_send)
    wait(kv.at[:, :, pl.ds(0, HALF), :], ga_send)
    wait(kv.at[:, :, pl.ds(0, 48), :], gz_send)
    wait(kv.at[:, :, pl.ds(0, 192), :], gx_send)
    wait(recv_a, ra_send)
    wait(recv_b, rb_send)
    wait(recv_d, rd_send)
    wait(recv_x, rx_send)
    wait(recv_z, rz_send)


def on_device(
    queries, out_grad, leaf_keys, leaf_values, mid_keys, mid_values, root_keys, root_values, mid_len, leaf_len
):
    vmem = pl.BlockSpec(memory_space=pltpu.VMEM)
    smem = pl.BlockSpec(memory_space=pltpu.SMEM)
    hbm = pl.BlockSpec(memory_space=pl.ANY)
    kvc = KVH * HD
    dma = pltpu.SemaphoreType.DMA
    one = dma(())
    each = dma((KVH,))
    return pl.pallas_call(
        kernel,
        out_shape=(
            jax.ShapeDtypeStruct((LEAF, QH * HD), BF),
            jax.ShapeDtypeStruct((LEAF, kvc), BF),
            jax.ShapeDtypeStruct((LEAF, kvc), BF),
            jax.ShapeDtypeStruct((16, kvc), F32),
            jax.ShapeDtypeStruct((16, kvc), F32),
            jax.ShapeDtypeStruct((2, kvc), F32),
            jax.ShapeDtypeStruct((2, kvc), F32),
        ),
        in_specs=[smem, smem, vmem, vmem, vmem, vmem, hbm, hbm, hbm, hbm],
        out_specs=(hbm, hbm, hbm, vmem, vmem, vmem, vmem),
        scratch_shapes=[
            pltpu.VMEM((KVH, 2, KEYS, HD), BF),
            pltpu.VMEM((LEAF, QH * HD), BF),
            pltpu.VMEM((LEAF, QH * HD), BF),
            pltpu.VMEM((LEAF, QH * HD), BF),
            pltpu.VMEM((LEAF, kvc), BF),
            pltpu.VMEM((LEAF, kvc), BF),
            pltpu.VMEM((8, MID), F32),
            pltpu.VMEM((LEAF, LEAF), F32),
            pltpu.VMEM((LEAF, HD), F32),
            pltpu.VMEM((GROUP, LEAF, KEYS), F32),
            pltpu.VMEM((GROUP, LEAF, KEYS), F32),
            pltpu.VMEM((GROUP * LEAF, KEYS), BF),
            pltpu.VMEM((GROUP * LEAF, KEYS), BF),
            pltpu.VMEM((2, 16, HD), BF),
            pltpu.VMEM((16, 2, 16, HD), BF),
            pltpu.VMEM((2, 256, HD), F32),
            pltpu.VMEM((KVH, 2, ROOT, HD), BF),
            pltpu.VMEM((KVH, 2, HALF, HD), BF),
            pltpu.VMEM((KVH, 2, HALF, HD), BF),
            pltpu.VMEM((KVH, 7, 2, 32, HD), BF),
            pltpu.VMEM((KVH, 2, MID, HD), BF),
            pltpu.VMEM((KVH, 3, 2, 64, HD), BF),
            pltpu.VMEM((KVH, 2, 64, HD), BF),
            pltpu.VMEM((KVH, 3, 2, 16, HD), BF),
            pltpu.VMEM((2, 256, HD), F32),
            pltpu.VMEM((16, 2, 16, HD), BF),
            pltpu.VMEM((15, 2, 16, HD), BF),
            each, each, each, dma((3,)),
            one, one, one, each, one, each, one, each, one, each,
            one, each, one, each, one, one, one, each, one, each,
        ],
        compiler_params=pltpu.CompilerParams(
            collective_id=0, has_side_effects=True, vmem_limit_bytes=60 * 1024 * 1024
        ),
        cost_estimate=pl.CostEstimate(flops=10 * 2**30, bytes_accessed=8 * 2**20, transcendentals=2**23),
    )(mid_len, leaf_len, root_keys, root_values, mid_keys, mid_values, queries, out_grad, leaf_keys, leaf_values)


def solution(mesh):
    both = P(("mid", "leaf"), None)
    return jax.shard_map(
        on_device,
        mesh=mesh,
        in_specs=(both,) * 8 + (P("mid"), P(("mid", "leaf"))),
        out_specs=(both,) * 7,
        check_vma=False,
    )
```

```python
import functools

import jax
import jax.numpy as jnp
from jax import lax
from jax.experimental import pallas as pl
from jax.experimental.pallas import tpu as pltpu
from jax.sharding import PartitionSpec as P

QH = 32
KVH = 8
HD = 128
GROUP = QH // KVH
LEAF = 256
MID = 256
ROOT = 512
KEYS = ROOT + MID + LEAF
HALF = ROOT // 2
OWN = ROOT + MID
CHUNK = 64
AHEAD = 2
DIRECT = 2
FACTOR = HD ** (-0.5)
LOG2E = 1.4426950408889634
MESH = pl.DeviceIdType.MESH
BF = jnp.bfloat16
F32 = jnp.float32


def nt(a, b):
    return lax.dot_general(a, b, (((1,), (1,)), ((), ())), preferred_element_type=F32)


def tn(a, b):
    return lax.dot_general(a, b, (((0,), (0,)), ((), ())), preferred_element_type=F32)


def kernel(
    mid_len, leaf_len, rk_hbm, rv_hbm, mk_hbm, mv_hbm, q_hbm, g_hbm, lk_hbm, lv_hbm,
    dqb, dlk, dlv, dmk, dmv, drk, drv,
    rk, rv, mk, mv, kv, qb, gb, bias_mid, bias_own, live, s_scr, dp_scr, p_scr, ds_scr,
    shard, gd, gf, rsend, recv_a, bsend, recv_b, recv_y, lsend, recv_l, msend, recv_x, zsend, recv_z, df, dsend, recv_d,
    load_s, load_q, load_g, load_kv,
    gd_send, gd_recv, gb_send, gb_recv, gl_send, gl_recv, gy_send, gy_recv, ga_send, ga_recv, gz_send, gz_recv,
    gx_send, gx_recv, ra_send, ra_recv, rb_send, rb_recv, ry_send, ry_recv, rl_send, rl_recv, rd_send, rd_recv,
    rx_send, rx_recv, rz_send, rz_recv,
):
    m = lax.axis_index("mid")
    l = lax.axis_index("leaf")
    core = lax.rem(m, 2)
    b = m // 2
    x = l // 4
    z = lax.rem(l, 4)
    y = m // 4
    zl = lax.rem(b, 2)

    def at(mm, ll):
        return {"mid": mm, "leaf": ll}

    sibling = at(m + 1 - 2 * core, l)
    next_z = at(m + 2 - 4 * zl, l)

    leaf_ids = {d: lax.rem(l + d, 16) for d in range(1, 16)}
    b_ids = {d: lax.rem(b + d, 8) for d in range(1, 8)}
    x_ids = {d: lax.rem(x + d, 4) for d in range(1, 4)}
    y_ids = {d: lax.rem(y + d, 4) for d in range(1, 4)}
    z_ids = {d: lax.rem(z + d, 4) for d in range(1, 4)}
    leaf_at = {d: at(m, leaf_ids[d]) for d in range(1, 16)}
    b_at = {d: at(b_ids[d] * 2 + core, l) for d in range(1, 8)}
    x_at = {d: at(m, x_ids[d] * 4 + z) for d in range(1, 4)}
    y_at = {d: at(y_ids[d] * 4 + zl * 2 + core, l) for d in range(1, 4)}
    z_at = {d: at(m, x * 4 + z_ids[d]) for d in range(1, 4)}
    b_rows = {d: pl.ds(pl.multiple_of(b_ids[d] * 32, 32), 32) for d in range(1, 8)}
    x_rows_of = {d: pl.ds(pl.multiple_of(x_ids[d] * 64, 64), 64) for d in range(1, 4)}
    y_rows_of = {d: pl.ds(pl.multiple_of(y_ids[d] * 64, 64), 64) for d in range(1, 4)}
    z_rows_of = {d: pl.ds(pl.multiple_of(z_ids[d] * 16, 16), 16) for d in range(1, 4)}
    own_b = pl.ds(pl.multiple_of(b * 32, 32), 32)
    own_x = pl.ds(pl.multiple_of(x * 64, 64), 64)
    own_y = pl.ds(pl.multiple_of(y * 64, 64), 64)
    own_z = pl.ds(pl.multiple_of(z * 16, 16), 16)
    own_l = pl.ds(pl.multiple_of(zl * 32, 32), 32)
    other_l = pl.ds(pl.multiple_of(32 - zl * 32, 32), 32)

    def send(src, dst, ssem, rsem, device):
        pltpu.make_async_remote_copy(
            src_ref=src, dst_ref=dst, send_sem=ssem, recv_sem=rsem,
            device_id=device, device_id_type=MESH,
        ).start()

    def wait(ref, sem):
        pltpu.make_async_copy(ref, ref, sem).wait()

    def cols(h, width):
        return pl.ds(pl.multiple_of(h * width, width), width)

    barrier = pltpu.get_barrier_semaphore()
    for d in range(1, 16):
        pl.semaphore_signal(barrier, inc=1, device_id=leaf_at[d], device_id_type=MESH)
    for d in range(1, 8):
        pl.semaphore_signal(barrier, inc=1, device_id=b_at[d], device_id_type=MESH)
    pl.semaphore_signal(barrier, inc=1, device_id=sibling, device_id_type=MESH)
    small = [
        pltpu.make_async_copy(src, dst, load_s.at[i])
        for i, (src, dst) in enumerate(((rk_hbm, rk), (rv_hbm, rv), (mk_hbm, mk), (mv_hbm, mv)))
    ]
    for copy in small:
        copy.start()
    for copy in small:
        copy.wait()

    for kind, ref in ((0, rk), (1, rv)):
        val = ref[...].astype(F32)
        for r in range(2):
            for h in range(KVH):
                gf[h // 4, pl.ds(kind * 8 + r * 4 + h % 4, 1), :] = val[r : r + 1, h * HD : (h + 1) * HD]
    for half in range(2):
        tile = gf[half, pl.ds(0, 16), :].astype(BF)
        shard[half] = tile
        gd[half, l] = tile
    mid_rows = pl.ds(pl.multiple_of(ROOT + l * 16, 16), 16)
    for kind, ref in ((0, mk), (1, mv)):
        for h in range(KVH):
            kv[h, kind, mid_rows, :] = ref[:, h * HD : (h + 1) * HD]

    pl.semaphore_wait(barrier, 23)

    def send_mid(h0, n, sem):
        part = kv.at[pl.ds(h0, n), :, mid_rows, :]
        for d in range(1, 4):
            send(part, part, gz_send, sem, z_at[d])

    for d in range(1, 16):
        send(shard.at[0], gd.at[0, l], gd_send, gd_recv.at[0], leaf_at[d])
    send_mid(0, DIRECT, gz_recv.at[0])
    for d in range(1, 16):
        send(shard.at[1], gd.at[1, l], gd_send, gd_recv.at[1], leaf_at[d])

    w = GROUP * HD
    for h in range(KVH):
        pltpu.make_async_copy(lk_hbm.at[:, cols(h, HD)], kv.at[h, 0, pl.ds(OWN, LEAF), :], load_kv.at[h]).start()
        pltpu.make_async_copy(lv_hbm.at[:, cols(h, HD)], kv.at[h, 1, pl.ds(OWN, LEAF), :], load_kv.at[h]).start()
        pltpu.make_async_copy(q_hbm.at[:, cols(h, w)], qb.at[:, cols(h, w)], load_q.at[h]).start()
        pltpu.make_async_copy(g_hbm.at[:, cols(h, w)], gb.at[:, cols(h, w)], load_g.at[h]).start()

    mlen = mid_len[0]
    llen = leaf_len[0]
    bias_mid[...] = jnp.where(lax.broadcasted_iota(jnp.int32, (8, MID), 1) < mlen, 0.0, -1e30)
    row = lax.broadcasted_iota(jnp.int32, (LEAF, LEAF), 0)
    col = lax.broadcasted_iota(jnp.int32, (LEAF, LEAF), 1)
    bias_own[...] = jnp.where((col <= row) & (col < llen), 0.0, -1e30)
    live[...] = jnp.where(lax.broadcasted_iota(jnp.int32, (LEAF, HD), 0) < llen, 1.0, 0.0)

    my_rows = pl.ds(pl.multiple_of(core * HALF + b * 32, 32), 32)
    y_rows = pl.ds(pl.multiple_of(core * HALF + y * 64, 64), 64)
    my_half = pl.ds(pl.multiple_of(core * HALF, HALF), HALF)
    other_half = pl.ds(pl.multiple_of((1 - core) * HALF, HALF), HALF)
    x_rows = pl.ds(pl.multiple_of(ROOT + x * 64, 64), 64)

    def unpack(half):
        wait(gd.at[half, pl.ds(0, 15)], gd_recv.at[half])
        gf[half] = gd[half].reshape(256, HD).astype(F32)
        for hh in range(4):
            for kind in range(2):
                kv[half * 4 + hh, kind, my_rows, :] = jnp.concatenate(
                    [gf[half, pl.ds(kind * 8 + r * 4 + hh, 16, stride=16), :] for r in range(2)], 0
                ).astype(BF)

    def share_mid(h0, n):
        part = kv.at[pl.ds(h0, n), :, x_rows, :]
        for d in range(1, 4):
            send(part, part, gx_send, gx_recv.at[h0 // 2], x_at[d])

    def share_half(h):
        part = kv.at[h, :, my_half, :]
        send(part, part, ga_send, ga_recv.at[h], sibling)

    unpack(0)
    for h in range(DIRECT):
        part = kv.at[h, :, my_rows, :]
        for d in range(1, 8):
            send(part, part, gb_send, gb_recv.at[h], b_at[d])
    unpack(1)
    part = kv.at[pl.ds(DIRECT, KVH - DIRECT), :, my_rows, :]
    send(part, part, gl_send, gl_recv, next_z)
    wait(kv.at[pl.ds(0, DIRECT), :, pl.ds(ROOT, 48), :], gz_recv.at[0])
    share_mid(0, 2)
    send_mid(DIRECT, KVH - DIRECT, gz_recv.at[1])
    for h in range(DIRECT):
        wait(kv.at[h, :, pl.ds(0, 224), :], gb_recv.at[h])
        share_half(h)

    def relay():
        wait(kv.at[pl.ds(DIRECT, KVH - DIRECT), :, pl.ds(0, 32), :], gl_recv)
        for h in range(DIRECT, KVH, 2):
            part = kv.at[pl.ds(h, 2), :, y_rows, :]
            for d in range(1, 4):
                send(part, part, gy_send, gy_recv.at[h // 2], y_at[d])
        wait(kv.at[pl.ds(DIRECT, KVH - DIRECT), :, pl.ds(ROOT, 48), :], gz_recv.at[1])
        for h in range(DIRECT, KVH, 2):
            share_mid(h, 2)

    def compute(h):
        keys = kv.at[h, 0]
        values = kv.at[h, 1]

        def head_cols(g):
            return pl.ds(pl.multiple_of(h * (GROUP * HD) + g * HD, HD), HD)

        def dots(g):
            s_scr[g] = nt(qb[:, head_cols(g)], keys[...])
            dp_scr[g] = nt(gb[:, head_cols(g)], values[...])

        def soft(g):
            for r0 in range(0, LEAF, CHUNK):
                rows = pl.ds(r0, CHUNK)
                out = pl.ds(g * LEAF + r0, CHUNK)
                s = s_scr[g, rows, :] * (FACTOR * LOG2E)
                s = jnp.concatenate(
                    [s[:, :ROOT], s[:, ROOT:OWN] + bias_mid[0:1, :], s[:, OWN:] + bias_own[rows, :]], 1
                )
                top = jnp.max(s, -1, keepdims=True)
                w = jnp.exp2(s - top)
                p = w * (live[rows, 0:1] / jnp.sum(w, -1, keepdims=True))
                p_scr[out, :] = p.astype(BF)
                dp = dp_scr[g, rows, :]
                dot = jnp.sum(p * dp, -1, keepdims=True)
                ds_scr[out, :] = (p * (dp - dot)).astype(BF)
            dq = jnp.dot(ds_scr[pl.ds(g * LEAF, LEAF), :], keys[...], preferred_element_type=F32)
            dqb[:, head_cols(g)] = (dq * FACTOR).astype(BF)

        dots(0)
        for g in range(GROUP):
            if g + 1 < GROUP:
                dots(g + 1)
            soft(g)
            if g == 0:
                pl.when(h == 0)(relay)
        qs = jnp.concatenate([qb[:, head_cols(g)] for g in range(GROUP)], 0)
        gs = jnp.concatenate([gb[:, head_cols(g)] for g in range(GROUP)], 0)
        dk = tn(qs, ds_scr[...]).T * FACTOR
        dv = tn(gs, p_scr[...]).T
        for kind, val, own in ((0, dk, dlk), (1, dv, dlv)):
            low = val.astype(BF)
            rsend[h, kind] = low[:ROOT]
            msend[h, kind] = low[ROOT:OWN]
            own[:, cols(h, HD)] = low[OWN:]

    def mid_first(p):
        for d in range(1, 4):
            src = msend.at[pl.ds(2 * p, 2), :, x_rows_of[d], :]
            send(src, recv_x.at[p, d - 1], rx_send, rx_recv.at[p], x_at[d])

    def half_sum(h):
        wait(recv_a.at[h], ra_recv.at[h])
        bsend[h] = (rsend[h, :, my_half, :].astype(F32) + recv_a[h].astype(F32)).astype(BF)

    def mid_second(p):
        wait(recv_x.at[p], rx_recv.at[p])
        pair = pl.ds(2 * p, 2)
        own = msend[pair, :, own_x, :].astype(F32)
        zsend[pair] = (own + jnp.sum(recv_x[p].astype(F32), 0)).astype(BF)
        for d in range(1, 4):
            src = zsend.at[pair, :, z_rows_of[d], :]
            send(src, recv_z.at[p, d - 1], rz_send, rz_recv.at[p], z_at[d])

    def mid_third(p):
        wait(recv_z.at[p], rz_recv.at[p])
        pair = pl.ds(2 * p, 2)
        own = zsend[pair, :, own_z, :].astype(F32)
        total = own + jnp.sum(recv_z[p].astype(F32), 0)
        for i in range(2):
            dmk[:, cols(2 * p + i, HD)] = total[i, 0]
            dmv[:, cols(2 * p + i, HD)] = total[i, 1]

    def keep_root(h, total):
        half = h // 4
        hh = lax.rem(h, 4)
        for kind in range(2):
            for r in range(2):
                df[half, pl.ds(kind * 8 + r * 4 + hh, 16, stride=16), :] = total[kind, r * 16 : (r + 1) * 16]

    def last_sends(half):
        dsend[half] = df[half].astype(BF).reshape(16, 16, HD)
        for d in range(1, 16):
            send(dsend.at[half, leaf_ids[d]], recv_d.at[half, d - 1], rd_send, rd_recv.at[half], leaf_at[d])

    def last_sums(half):
        wait(recv_d.at[half], rd_recv.at[half])
        total = dsend[half, l].astype(F32) + jnp.sum(recv_d[half].astype(F32), 0)
        for kind, ref in ((0, drk), (1, drv)):
            for r in range(2):
                for hh in range(4):
                    row = kind * 8 + r * 4 + hh
                    h = half * 4 + hh
                    ref[r : r + 1, h * HD : (h + 1) * HD] = total[row : row + 1]

    def root_second(h):
        half_sum(h)
        for d in range(1, 4):
            src = bsend.at[h, :, y_rows_of[d], :]
            send(src, recv_y.at[h, d - 1], ry_send, ry_recv.at[h], y_at[d])

    def root_third(h):
        wait(recv_y.at[h], ry_recv.at[h])
        own = bsend[h, :, own_y, :].astype(F32)
        lsend[h] = (own + jnp.sum(recv_y[h].astype(F32), 0)).astype(BF)
        src = lsend.at[h, :, other_l, :]
        send(src, recv_l.at[h], rl_send, rl_recv.at[h], next_z)

    def root_fourth(h):
        wait(recv_l.at[h], rl_recv.at[h])
        own = lsend[h, :, own_l, :].astype(F32)
        keep_root(h, own + recv_l[h].astype(F32))

    def root_second_direct(h):
        half_sum(h)
        at_h = h - (KVH - DIRECT)
        for d in range(1, 8):
            src = bsend.at[h, :, b_rows[d], :]
            send(src, recv_b.at[at_h, d - 1], rb_send, rb_recv.at[at_h], b_at[d])

    def root_third_direct(h):
        at_h = h - (KVH - DIRECT)
        wait(recv_b.at[at_h], rb_recv.at[at_h])
        own = bsend[h, :, own_b, :].astype(F32)
        keep_root(h, own + jnp.sum(recv_b[at_h].astype(F32), 0))

    def step(h, carry):
        wait(qb.at[:, cols(h, GROUP * HD)], load_q.at[h])
        wait(gb.at[:, cols(h, GROUP * HD)], load_g.at[h])
        wait(kv.at[h, :, pl.ds(OWN, LEAF), :], load_kv.at[h])
        wait(kv.at[h, :, pl.ds(0, HALF), :], ga_recv.at[h])

        @pl.when(lax.rem(h, 2) == 0)
        def _():
            wait(kv.at[pl.ds(0, 2), :, pl.ds(0, 192), :], gx_recv.at[h // 2])

        compute(h)
        send(rsend.at[h, :, other_half, :], recv_a.at[h], ra_send, ra_recv.at[h], sibling)

        @pl.when(h + AHEAD < KVH)
        def _():
            @pl.when(lax.rem(h, 2) == 0)
            def _():
                wait(kv.at[pl.ds(0, 2), :, pl.ds(0, 192), :], gy_recv.at[h // 2 + 1])

            share_half(h + AHEAD)

        @pl.when(lax.rem(h, 2) == 1)
        def _():
            mid_first(h // 2)

        @pl.when((h >= 1) & (h < KVH - 1))
        def _():
            root_second(h - 1)

        @pl.when((h >= 2) & (lax.rem(h, 2) == 0))
        def _():
            mid_second(h // 2 - 1)

        @pl.when(h >= 2)
        def _():
            root_third(h - 2)

        @pl.when((h >= 3) & (lax.rem(h, 2) == 1))
        def _():
            mid_third(h // 2 - 1)

        @pl.when(h >= 3)
        def _():
            root_fourth(h - 3)

        @pl.when(h == 6)
        def _():
            last_sends(0)

        return carry

    lax.fori_loop(0, KVH, step, 0)
    root_second_direct(KVH - 2)
    root_second_direct(KVH - 1)
    mid_second(3)
    root_fourth(KVH - 3)
    root_third_direct(KVH - 2)
    last_sums(0)
    root_third_direct(KVH - 1)
    last_sends(1)
    mid_third(3)
    last_sums(1)

    wait(gd.at[:, pl.ds(0, 15)], gd_send)
    wait(kv.at[pl.ds(0, DIRECT), :, pl.ds(0, 224), :], gb_send)
    wait(kv.at[pl.ds(0, KVH - DIRECT), :, pl.ds(0, 32), :], gl_send)
    wait(kv.at[pl.ds(0, KVH - DIRECT), :, pl.ds(0, 192), :], gy_send)
    wait(kv.at[:, :, pl.ds(0, HALF), :], ga_send)
    wait(kv.at[:, :, pl.ds(0, 48), :], gz_send)
    wait(kv.at[:, :, pl.ds(0, 192), :], gx_send)
    wait(recv_a, ra_send)
    wait(recv_b, rb_send)
    wait(recv_y, ry_send)
    wait(recv_l, rl_send)
    wait(recv_d, rd_send)
    wait(recv_x, rx_send)
    wait(recv_z, rz_send)


OUTS = (
    ((LEAF, QH * HD), BF),
    ((LEAF, KVH * HD), BF),
    ((LEAF, KVH * HD), BF),
    ((16, KVH * HD), F32),
    ((16, KVH * HD), F32),
    ((2, KVH * HD), F32),
    ((2, KVH * HD), F32),
)


def place(*refs):
    sems = refs[-1]
    copies = [pltpu.make_async_copy(refs[i], refs[7 + i], sems.at[i]) for i in range(7)]
    for c in copies:
        c.start()
    for c in copies:
        c.wait()


def on_device(
    queries, out_grad, leaf_keys, leaf_values, mid_keys, mid_values, root_keys, root_values, mid_len, leaf_len
):
    vmem = pl.BlockSpec(memory_space=pltpu.VMEM)
    smem = pl.BlockSpec(memory_space=pltpu.SMEM)
    hbm = pl.BlockSpec(memory_space=pl.ANY)
    kvc = KVH * HD
    dma = pltpu.SemaphoreType.DMA
    one = dma(())
    two = dma((2,))
    each = dma((KVH,))
    outs = pl.pallas_call(
        kernel,
        out_shape=tuple(pltpu.VMEM(*o) for o in OUTS),
        in_specs=[smem, smem] + [hbm] * 8,
        out_specs=(vmem,) * 7,
        scratch_shapes=[
            pltpu.VMEM((2, kvc), BF),
            pltpu.VMEM((2, kvc), BF),
            pltpu.VMEM((16, kvc), BF),
            pltpu.VMEM((16, kvc), BF),
            pltpu.VMEM((KVH, 2, KEYS, HD), BF),
            pltpu.VMEM((LEAF, QH * HD), BF),
            pltpu.VMEM((LEAF, QH * HD), BF),
            pltpu.VMEM((8, MID), F32),
            pltpu.VMEM((LEAF, LEAF), F32),
            pltpu.VMEM((LEAF, HD), F32),
            pltpu.VMEM((GROUP, LEAF, KEYS), F32),
            pltpu.VMEM((GROUP, LEAF, KEYS), F32),
            pltpu.VMEM((GROUP * LEAF, KEYS), BF),
            pltpu.VMEM((GROUP * LEAF, KEYS), BF),
            pltpu.VMEM((2, 16, HD), BF),
            pltpu.VMEM((2, 16, 16, HD), BF),
            pltpu.VMEM((2, 256, HD), F32),
            pltpu.VMEM((KVH, 2, ROOT, HD), BF),
            pltpu.VMEM((KVH, 2, HALF, HD), BF),
            pltpu.VMEM((KVH, 2, HALF, HD), BF),
            pltpu.VMEM((DIRECT, 7, 2, 32, HD), BF),
            pltpu.VMEM((KVH - DIRECT, 3, 2, 64, HD), BF),
            pltpu.VMEM((KVH - DIRECT, 2, 64, HD), BF),
            pltpu.VMEM((KVH - DIRECT, 2, 32, HD), BF),
            pltpu.VMEM((KVH, 2, MID, HD), BF),
            pltpu.VMEM((KVH // 2, 3, 2, 2, 64, HD), BF),
            pltpu.VMEM((KVH, 2, 64, HD), BF),
            pltpu.VMEM((KVH // 2, 3, 2, 2, 16, HD), BF),
            pltpu.VMEM((2, 256, HD), F32),
            pltpu.VMEM((2, 16, 16, HD), BF),
            pltpu.VMEM((2, 15, 16, HD), BF),
            dma((4,)), each, each, each,
            one, two, one, each, one, one, one, each, one, each, one, two,
            one, each, one, each, one, each, one, each, one, each, one, two,
            one, each, one, each,
        ],
        compiler_params=pltpu.CompilerParams(
            collective_id=0, has_side_effects=True, vmem_limit_bytes=60 * 1024 * 1024
        ),
        cost_estimate=pl.CostEstimate(flops=10 * 2**30, bytes_accessed=8 * 2**20, transcendentals=2**23),
    )(mid_len, leaf_len, root_keys, root_values, mid_keys, mid_values, queries, out_grad, leaf_keys, leaf_values)
    return pl.pallas_call(
        place,
        out_shape=tuple(jax.ShapeDtypeStruct(*o) for o in OUTS),
        in_specs=[vmem] * 7,
        out_specs=(hbm,) * 7,
        scratch_shapes=[dma((7,))],
        compiler_params=pltpu.CompilerParams(vmem_limit_bytes=4 * 1024 * 1024),
    )(*outs)


def solution(mesh):
    both = P(("mid", "leaf"), None)
    return jax.shard_map(
        on_device,
        mesh=mesh,
        in_specs=(both,) * 8 + (P("mid"), P(("mid", "leaf"))),
        out_specs=(both,) * 7,
        check_vma=False,
    )
```

```python
import functools

import jax
import jax.numpy as jnp
from jax import lax
from jax.experimental import pallas as pl
from jax.experimental.pallas import tpu as pltpu
from jax.sharding import PartitionSpec as P

QH = 32
KVH = 8
HD = 128
GROUP = QH // KVH
LEAF = 256
MID = 256
ROOT = 512
KEYS = ROOT + MID + LEAF
HALF = ROOT // 2
OWN = ROOT + MID
CHUNK = 64
AHEAD = 2
DIRECT = 2
FACTOR = HD ** (-0.5)
LOG2E = 1.4426950408889634
MESH = pl.DeviceIdType.MESH
BF = jnp.bfloat16
F32 = jnp.float32


def nt(a, b):
    return lax.dot_general(a, b, (((1,), (1,)), ((), ())), preferred_element_type=F32)


def tn(a, b):
    return lax.dot_general(a, b, (((0,), (0,)), ((), ())), preferred_element_type=F32)


def kernel(
    mid_len, leaf_len, rk_hbm, rv_hbm, mk_hbm, mv_hbm, q_hbm, g_hbm, lk_hbm, lv_hbm,
    dqb, dlk, dlv, dmk, dmv, drk, drv,
    rk, rv, mk, mv, kv, qb, gb, bias_mid, bias_own, live, s_scr, dp_scr, p_scr, ds_all,
    shard, gd, gf, rsend, recv_a, bsend, recv_b, recv_y, lsend, recv_l, msend, recv_x, zsend, recv_z, df, dsend, recv_d,
    load_s, load_q, load_g, load_kv,
    gd_send, gd_recv, gb_send, gb_recv, gl_send, gl_recv, gy_send, gy_recv, ga_send, ga_recv, gz_send, gz_recv,
    gx_send, gx_recv, ra_send, ra_recv, rb_send, rb_recv, ry_send, ry_recv, rl_send, rl_recv, rd_send, rd_recv,
    rx_send, rx_recv, rz_send, rz_recv,
):
    m = lax.axis_index("mid")
    l = lax.axis_index("leaf")
    core = lax.rem(m, 2)
    b = m // 2
    x = l // 4
    z = lax.rem(l, 4)
    y = m // 4
    zl = lax.rem(b, 2)

    def at(mm, ll):
        return {"mid": mm, "leaf": ll}

    sibling = at(m + 1 - 2 * core, l)
    next_z = at(m + 2 - 4 * zl, l)

    leaf_ids = {d: lax.rem(l + d, 16) for d in range(1, 16)}
    b_ids = {d: lax.rem(b + d, 8) for d in range(1, 8)}
    x_ids = {d: lax.rem(x + d, 4) for d in range(1, 4)}
    y_ids = {d: lax.rem(y + d, 4) for d in range(1, 4)}
    z_ids = {d: lax.rem(z + d, 4) for d in range(1, 4)}
    leaf_at = {d: at(m, leaf_ids[d]) for d in range(1, 16)}
    b_at = {d: at(b_ids[d] * 2 + core, l) for d in range(1, 8)}
    x_at = {d: at(m, x_ids[d] * 4 + z) for d in range(1, 4)}
    y_at = {d: at(y_ids[d] * 4 + zl * 2 + core, l) for d in range(1, 4)}
    z_at = {d: at(m, x * 4 + z_ids[d]) for d in range(1, 4)}
    b_rows = {d: pl.ds(pl.multiple_of(b_ids[d] * 32, 32), 32) for d in range(1, 8)}
    x_rows_of = {d: pl.ds(pl.multiple_of(x_ids[d] * 64, 64), 64) for d in range(1, 4)}
    y_rows_of = {d: pl.ds(pl.multiple_of(y_ids[d] * 64, 64), 64) for d in range(1, 4)}
    z_rows_of = {d: pl.ds(pl.multiple_of(z_ids[d] * 16, 16), 16) for d in range(1, 4)}
    own_b = pl.ds(pl.multiple_of(b * 32, 32), 32)
    own_x = pl.ds(pl.multiple_of(x * 64, 64), 64)
    own_y = pl.ds(pl.multiple_of(y * 64, 64), 64)
    own_z = pl.ds(pl.multiple_of(z * 16, 16), 16)
    own_l = pl.ds(pl.multiple_of(zl * 32, 32), 32)
    other_l = pl.ds(pl.multiple_of(32 - zl * 32, 32), 32)

    def send(src, dst, ssem, rsem, device):
        pltpu.make_async_remote_copy(
            src_ref=src, dst_ref=dst, send_sem=ssem, recv_sem=rsem,
            device_id=device, device_id_type=MESH,
        ).start()

    def wait(ref, sem):
        pltpu.make_async_copy(ref, ref, sem).wait()

    def cols(h, width):
        return pl.ds(pl.multiple_of(h * width, width), width)

    barrier = pltpu.get_barrier_semaphore()
    for d in range(1, 16):
        pl.semaphore_signal(barrier, inc=1, device_id=leaf_at[d], device_id_type=MESH)
    for d in range(1, 8):
        pl.semaphore_signal(barrier, inc=1, device_id=b_at[d], device_id_type=MESH)
    pl.semaphore_signal(barrier, inc=1, device_id=sibling, device_id_type=MESH)
    small = [
        pltpu.make_async_copy(src, dst, load_s.at[i])
        for i, (src, dst) in enumerate(((rk_hbm, rk), (rv_hbm, rv), (mk_hbm, mk), (mv_hbm, mv)))
    ]
    for copy in small:
        copy.start()
    for copy in small:
        copy.wait()

    for kind, ref in ((0, rk), (1, rv)):
        val = ref[...].astype(F32)
        for r in range(2):
            for h in range(KVH):
                gf[h // 4, pl.ds(kind * 8 + r * 4 + h % 4, 1), :] = val[r : r + 1, h * HD : (h + 1) * HD]
    for half in range(2):
        tile = gf[half, pl.ds(0, 16), :].astype(BF)
        shard[half] = tile
        gd[half, l] = tile
    mid_rows = pl.ds(pl.multiple_of(ROOT + l * 16, 16), 16)
    for kind, ref in ((0, mk), (1, mv)):
        for h in range(KVH):
            kv[h, kind, mid_rows, :] = ref[:, h * HD : (h + 1) * HD]

    pl.semaphore_wait(barrier, 23)

    def send_mid(h0, n, sem):
        part = kv.at[pl.ds(h0, n), :, mid_rows, :]
        for d in range(1, 4):
            send(part, part, gz_send, sem, z_at[d])

    for d in range(1, 16):
        send(shard.at[0], gd.at[0, l], gd_send, gd_recv.at[0], leaf_at[d])
    send_mid(0, DIRECT, gz_recv.at[0])
    for d in range(1, 16):
        send(shard.at[1], gd.at[1, l], gd_send, gd_recv.at[1], leaf_at[d])

    w = GROUP * HD
    for h in range(KVH):
        pltpu.make_async_copy(lk_hbm.at[:, cols(h, HD)], kv.at[h, 0, pl.ds(OWN, LEAF), :], load_kv.at[h]).start()
        pltpu.make_async_copy(lv_hbm.at[:, cols(h, HD)], kv.at[h, 1, pl.ds(OWN, LEAF), :], load_kv.at[h]).start()
        pltpu.make_async_copy(q_hbm.at[:, cols(h, w)], qb.at[:, cols(h, w)], load_q.at[h]).start()
        pltpu.make_async_copy(g_hbm.at[:, cols(h, w)], gb.at[:, cols(h, w)], load_g.at[h]).start()

    for g in range(GROUP):
        p_scr[pl.ds(g * LEAF, HD), pl.ds(KEYS - HD, HD)] = jnp.zeros((HD, HD), BF)
        for h in range(KVH):
            ds_all[h, pl.ds(g * LEAF, HD), pl.ds(KEYS - HD, HD)] = jnp.zeros((HD, HD), BF)

    mlen = mid_len[0]
    llen = leaf_len[0]
    bias_mid[...] = jnp.where(lax.broadcasted_iota(jnp.int32, (8, MID), 1) < mlen, 0.0, -1e30)
    row = lax.broadcasted_iota(jnp.int32, (LEAF, LEAF), 0)
    col = lax.broadcasted_iota(jnp.int32, (LEAF, LEAF), 1)
    bias_own[...] = jnp.where((col <= row) & (col < llen), 0.0, -1e30)
    live[...] = jnp.where(lax.broadcasted_iota(jnp.int32, (LEAF, HD), 0) < llen, 1.0, 0.0)

    my_rows = pl.ds(pl.multiple_of(core * HALF + b * 32, 32), 32)
    y_rows = pl.ds(pl.multiple_of(core * HALF + y * 64, 64), 64)
    my_half = pl.ds(pl.multiple_of(core * HALF, HALF), HALF)
    other_half = pl.ds(pl.multiple_of((1 - core) * HALF, HALF), HALF)
    x_rows = pl.ds(pl.multiple_of(ROOT + x * 64, 64), 64)

    def unpack(half):
        wait(gd.at[half, pl.ds(0, 15)], gd_recv.at[half])
        gf[half, pl.ds(0, 256), :] = gd[half].reshape(256, HD).astype(F32)
        for hh in range(4):
            for kind in range(2):
                kv[half * 4 + hh, kind, my_rows, :] = jnp.concatenate(
                    [gf[half, pl.ds(kind * 8 + r * 4 + hh, 16, stride=16), :] for r in range(2)], 0
                ).astype(BF)

    def share_mid(h0, n):
        part = kv.at[pl.ds(h0, n), :, x_rows, :]
        for d in range(1, 4):
            send(part, part, gx_send, gx_recv.at[h0 // 2], x_at[d])

    def share_half(h):
        part = kv.at[h, :, my_half, :]
        send(part, part, ga_send, ga_recv.at[h], sibling)

    unpack(0)
    for h in range(DIRECT):
        part = kv.at[h, :, my_rows, :]
        for d in range(1, 8):
            send(part, part, gb_send, gb_recv.at[h], b_at[d])
    unpack(1)
    part = kv.at[pl.ds(DIRECT, KVH - DIRECT), :, my_rows, :]
    send(part, part, gl_send, gl_recv, next_z)
    wait(kv.at[pl.ds(0, DIRECT), :, pl.ds(ROOT, 48), :], gz_recv.at[0])
    share_mid(0, 2)
    send_mid(DIRECT, KVH - DIRECT, gz_recv.at[1])
    for h in range(DIRECT):
        wait(kv.at[h, :, pl.ds(0, 224), :], gb_recv.at[h])
        share_half(h)

    def relay():
        wait(kv.at[pl.ds(DIRECT, KVH - DIRECT), :, pl.ds(0, 32), :], gl_recv)
        for h in range(DIRECT, KVH, 2):
            part = kv.at[pl.ds(h, 2), :, y_rows, :]
            for d in range(1, 4):
                send(part, part, gy_send, gy_recv.at[h // 2], y_at[d])
        wait(kv.at[pl.ds(DIRECT, KVH - DIRECT), :, pl.ds(ROOT, 48), :], gz_recv.at[1])
        for h in range(DIRECT, KVH, 2):
            share_mid(h, 2)

    def compute(h):
        ds_scr = ds_all.at[h]
        keys = kv.at[h, 0]
        values = kv.at[h, 1]

        def head_cols(g):
            return pl.ds(pl.multiple_of(h * (GROUP * HD) + g * HD, HD), HD)

        def dots(g):
            s_scr[g] = nt(qb[:, head_cols(g)], keys[...])
            dp_scr[g] = nt(gb[:, head_cols(g)], values[...])

        def soft(g):
            for r0 in range(0, LEAF, CHUNK):
                rows = pl.ds(r0, CHUNK)
                out = pl.ds(g * LEAF + r0, CHUNK)
                width = KEYS if r0 + CHUNK > HD else KEYS - HD
                used = pl.ds(0, width)
                s = s_scr[g, rows, used] * (FACTOR * LOG2E)
                s = jnp.concatenate(
                    [s[:, :ROOT], s[:, ROOT:OWN] + bias_mid[0:1, :], s[:, OWN:] + bias_own[rows, 0 : width - OWN]], 1
                )
                top = jnp.max(s, -1, keepdims=True)
                w = jnp.exp2(s - top)
                p = w * (live[rows, 0:1] / jnp.sum(w, -1, keepdims=True))
                p_scr[out, used] = p.astype(BF)
                dp = dp_scr[g, rows, used]
                dot = jnp.sum(p * dp, -1, keepdims=True)
                ds_scr[out, used] = (p * (dp - dot)).astype(BF)

        dots(0)
        for g in range(GROUP):
            if g + 1 < GROUP:
                dots(g + 1)
            soft(g)
            if g == 0:
                pl.when(h == 0)(relay)
        qs = jnp.concatenate([qb[:, head_cols(g)] for g in range(GROUP)], 0)
        gs = jnp.concatenate([gb[:, head_cols(g)] for g in range(GROUP)], 0)
        dk = tn(qs, ds_scr[...]).T * FACTOR
        dv = tn(gs, p_scr[...]).T
        for kind, val, own in ((0, dk, dlk), (1, dv, dlv)):
            low = val.astype(BF)
            rsend[h, kind] = low[:ROOT]
            msend[h, kind] = low[ROOT:OWN]
            own[:, cols(h, HD)] = low[OWN:]

    def query_grads(first, last):
        def one(h, carry):
            for g in range(GROUP):
                dq = jnp.dot(ds_all[h, pl.ds(g * LEAF, LEAF), :], kv[h, 0], preferred_element_type=F32)
                out = pl.ds(pl.multiple_of(h * (GROUP * HD) + g * HD, HD), HD)
                dqb[:, out] = (dq * FACTOR).astype(BF)
            return carry

        lax.fori_loop(first, last, one, 0)

    def mid_first(p):
        for d in range(1, 4):
            src = msend.at[pl.ds(2 * p, 2), :, x_rows_of[d], :]
            send(src, recv_x.at[p, d - 1], rx_send, rx_recv.at[p], x_at[d])

    def half_sum(h):
        wait(recv_a.at[h], ra_recv.at[h])
        bsend[h] = (rsend[h, :, my_half, :].astype(F32) + recv_a[h].astype(F32)).astype(BF)

    def mid_second(p):
        wait(recv_x.at[p], rx_recv.at[p])
        pair = pl.ds(2 * p, 2)
        own = msend[pair, :, own_x, :].astype(F32)
        zsend[pair] = (own + jnp.sum(recv_x[p].astype(F32), 0)).astype(BF)
        for d in range(1, 4):
            src = zsend.at[pair, :, z_rows_of[d], :]
            send(src, recv_z.at[p, d - 1], rz_send, rz_recv.at[p], z_at[d])

    def mid_third(p):
        wait(recv_z.at[p], rz_recv.at[p])
        pair = pl.ds(2 * p, 2)
        own = zsend[pair, :, own_z, :].astype(F32)
        total = own + jnp.sum(recv_z[p].astype(F32), 0)
        for i in range(2):
            dmk[:, cols(2 * p + i, HD)] = total[i, 0]
            dmv[:, cols(2 * p + i, HD)] = total[i, 1]

    def keep_root(h, total):
        half = h // 4
        hh = lax.rem(h, 4)
        for kind in range(2):
            for r in range(2):
                df[half, pl.ds(kind * 8 + r * 4 + hh, 16, stride=16), :] = total[kind, r * 16 : (r + 1) * 16]

    def last_sends(half):
        dsend[half] = df[half, pl.ds(0, 256), :].astype(BF).reshape(16, 16, HD)
        for d in range(1, 16):
            send(dsend.at[half, leaf_ids[d]], recv_d.at[half, d - 1], rd_send, rd_recv.at[half], leaf_at[d])

    def last_sums(half):
        wait(recv_d.at[half], rd_recv.at[half])
        total = dsend[half, l].astype(F32) + jnp.sum(recv_d[half].astype(F32), 0)
        for kind, ref in ((0, drk), (1, drv)):
            for r in range(2):
                for hh in range(4):
                    row = kind * 8 + r * 4 + hh
                    h = half * 4 + hh
                    ref[r : r + 1, h * HD : (h + 1) * HD] = total[row : row + 1]

    def root_second(h):
        half_sum(h)
        for d in range(1, 4):
            src = bsend.at[h, :, y_rows_of[d], :]
            send(src, recv_y.at[h, d - 1], ry_send, ry_recv.at[h], y_at[d])

    def root_third(h):
        wait(recv_y.at[h], ry_recv.at[h])
        own = bsend[h, :, own_y, :].astype(F32)
        lsend[h] = (own + jnp.sum(recv_y[h].astype(F32), 0)).astype(BF)
        src = lsend.at[h, :, other_l, :]
        send(src, recv_l.at[h], rl_send, rl_recv.at[h], next_z)

    def root_fourth(h):
        wait(recv_l.at[h], rl_recv.at[h])
        own = lsend[h, :, own_l, :].astype(F32)
        keep_root(h, own + recv_l[h].astype(F32))

    def root_second_direct(h):
        half_sum(h)
        at_h = h - (KVH - DIRECT)
        for d in range(1, 8):
            src = bsend.at[h, :, b_rows[d], :]
            send(src, recv_b.at[at_h, d - 1], rb_send, rb_recv.at[at_h], b_at[d])

    def root_third_direct(h):
        at_h = h - (KVH - DIRECT)
        wait(recv_b.at[at_h], rb_recv.at[at_h])
        own = bsend[h, :, own_b, :].astype(F32)
        keep_root(h, own + jnp.sum(recv_b[at_h].astype(F32), 0))

    def step(h, carry):
        wait(qb.at[:, cols(h, GROUP * HD)], load_q.at[h])
        wait(gb.at[:, cols(h, GROUP * HD)], load_g.at[h])
        wait(kv.at[h, :, pl.ds(OWN, LEAF), :], load_kv.at[h])
        wait(kv.at[h, :, pl.ds(0, HALF), :], ga_recv.at[h])

        @pl.when(lax.rem(h, 2) == 0)
        def _():
            wait(kv.at[pl.ds(0, 2), :, pl.ds(0, 192), :], gx_recv.at[h // 2])

        compute(h)
        send(rsend.at[h, :, other_half, :], recv_a.at[h], ra_send, ra_recv.at[h], sibling)

        @pl.when(h + AHEAD < KVH)
        def _():
            @pl.when(lax.rem(h, 2) == 0)
            def _():
                wait(kv.at[pl.ds(0, 2), :, pl.ds(0, 192), :], gy_recv.at[h // 2 + 1])

            share_half(h + AHEAD)

        @pl.when(lax.rem(h, 2) == 1)
        def _():
            mid_first(h // 2)

        @pl.when((h >= 1) & (h < KVH - 1))
        def _():
            root_second(h - 1)

        @pl.when((h >= 2) & (lax.rem(h, 2) == 0))
        def _():
            mid_second(h // 2 - 1)

        @pl.when(h >= 2)
        def _():
            root_third(h - 2)

        @pl.when((h >= 3) & (lax.rem(h, 2) == 1))
        def _():
            mid_third(h // 2 - 1)

        @pl.when(h >= 3)
        def _():
            root_fourth(h - 3)

        @pl.when(h == 6)
        def _():
            last_sends(0)

        return carry

    lax.fori_loop(0, KVH, step, 0)
    root_second_direct(KVH - 2)
    query_grads(0, 1)
    root_second_direct(KVH - 1)
    mid_second(3)
    root_fourth(KVH - 3)
    query_grads(1, 5)
    root_third_direct(KVH - 2)
    last_sums(0)
    root_third_direct(KVH - 1)
    last_sends(1)
    query_grads(5, KVH)
    mid_third(3)
    last_sums(1)

    wait(gd.at[:, pl.ds(0, 15)], gd_send)
    wait(kv.at[pl.ds(0, DIRECT), :, pl.ds(0, 224), :], gb_send)
    wait(kv.at[pl.ds(0, KVH - DIRECT), :, pl.ds(0, 32), :], gl_send)
    wait(kv.at[pl.ds(0, KVH - DIRECT), :, pl.ds(0, 192), :], gy_send)
    wait(kv.at[:, :, pl.ds(0, HALF), :], ga_send)
    wait(kv.at[:, :, pl.ds(0, 48), :], gz_send)
    wait(kv.at[:, :, pl.ds(0, 192), :], gx_send)
    wait(recv_a, ra_send)
    wait(recv_b, rb_send)
    wait(recv_y, ry_send)
    wait(recv_l, rl_send)
    wait(recv_d, rd_send)
    wait(recv_x, rx_send)
    wait(recv_z, rz_send)


OUTS = (
    ((LEAF, QH * HD), BF),
    ((LEAF, KVH * HD), BF),
    ((LEAF, KVH * HD), BF),
    ((16, KVH * HD), F32),
    ((16, KVH * HD), F32),
    ((2, KVH * HD), F32),
    ((2, KVH * HD), F32),
)


def place(*refs):
    sems = refs[-1]
    copies = [pltpu.make_async_copy(refs[i], refs[7 + i], sems.at[i]) for i in range(7)]
    for c in copies:
        c.start()
    for c in copies:
        c.wait()


def on_device(
    queries, out_grad, leaf_keys, leaf_values, mid_keys, mid_values, root_keys, root_values, mid_len, leaf_len
):
    vmem = pl.BlockSpec(memory_space=pltpu.VMEM)
    smem = pl.BlockSpec(memory_space=pltpu.SMEM)
    hbm = pl.BlockSpec(memory_space=pl.ANY)
    kvc = KVH * HD
    dma = pltpu.SemaphoreType.DMA
    one = dma(())
    two = dma((2,))
    each = dma((KVH,))
    outs = pl.pallas_call(
        kernel,
        out_shape=tuple(pltpu.VMEM(*o) for o in OUTS),
        in_specs=[smem, smem] + [hbm] * 8,
        out_specs=(vmem,) * 7,
        scratch_shapes=[
            pltpu.VMEM((2, kvc), BF),
            pltpu.VMEM((2, kvc), BF),
            pltpu.VMEM((16, kvc), BF),
            pltpu.VMEM((16, kvc), BF),
            pltpu.VMEM((KVH, 2, KEYS, HD), BF),
            pltpu.VMEM((LEAF, QH * HD), BF),
            pltpu.VMEM((LEAF, QH * HD), BF),
            pltpu.VMEM((8, MID), F32),
            pltpu.VMEM((LEAF, LEAF), F32),
            pltpu.VMEM((LEAF, HD), F32),
            pltpu.VMEM((GROUP, LEAF, KEYS), F32),
            pltpu.VMEM((GROUP, LEAF, KEYS), F32),
            pltpu.VMEM((GROUP * LEAF, KEYS), BF),
            pltpu.VMEM((KVH, GROUP * LEAF, KEYS), BF),
            pltpu.VMEM((2, 16, HD), BF),
            pltpu.VMEM((2, 16, 16, HD), BF),
            pltpu.VMEM((2, 272, HD), F32),
            pltpu.VMEM((KVH, 2, ROOT, HD), BF),
            pltpu.VMEM((KVH, 2, HALF, HD), BF),
            pltpu.VMEM((KVH, 2, HALF, HD), BF),
            pltpu.VMEM((DIRECT, 7, 2, 32, HD), BF),
            pltpu.VMEM((KVH - DIRECT, 3, 2, 64, HD), BF),
            pltpu.VMEM((KVH - DIRECT, 2, 64, HD), BF),
            pltpu.VMEM((KVH - DIRECT, 2, 32, HD), BF),
            pltpu.VMEM((KVH, 2, MID, HD), BF),
            pltpu.VMEM((KVH // 2, 3, 2, 2, 64, HD), BF),
            pltpu.VMEM((KVH, 2, 64, HD), BF),
            pltpu.VMEM((KVH // 2, 3, 2, 2, 16, HD), BF),
            pltpu.VMEM((2, 272, HD), F32),
            pltpu.VMEM((2, 16, 16, HD), BF),
            pltpu.VMEM((2, 15, 16, HD), BF),
            dma((4,)), each, each, each,
            one, two, one, each, one, one, one, each, one, each, one, two,
            one, each, one, each, one, each, one, each, one, each, one, two,
            one, each, one, each,
        ],
        compiler_params=pltpu.CompilerParams(
            collective_id=0, has_side_effects=True, vmem_limit_bytes=60 * 1024 * 1024
        ),
        cost_estimate=pl.CostEstimate(flops=10 * 2**30, bytes_accessed=8 * 2**20, transcendentals=2**23),
    )(mid_len, leaf_len, root_keys, root_values, mid_keys, mid_values, queries, out_grad, leaf_keys, leaf_values)
    return pl.pallas_call(
        place,
        out_shape=tuple(jax.ShapeDtypeStruct(*o) for o in OUTS),
        in_specs=[vmem] * 7,
        out_specs=(hbm,) * 7,
        scratch_shapes=[dma((7,))],
        compiler_params=pltpu.CompilerParams(vmem_limit_bytes=4 * 1024 * 1024),
    )(*outs)


def solution(mesh):
    both = P(("mid", "leaf"), None)
    return jax.shard_map(
        on_device,
        mesh=mesh,
        in_specs=(both,) * 8 + (P("mid"), P(("mid", "leaf"))),
        out_specs=(both,) * 7,
        check_vma=False,
    )
```
